512 devices in a mesh: tile: 128 (over z, y, core), head: 4 (over x).
Axes of the slice: x: 4, y: 4, z: 16, core: 2. Of those that a mesh axis runs over, the one named last changes fastest.
Arguments:
- grid_tokens: bfloat16 [65536, 768], P('tile')
- obs_tokens: bfloat16 [65536, 768], P('tile')
- w_query: bfloat16 [768, 768], P(None, 'head'), may hold values from -0.21875 to 0.21875
- w_gridval: bfloat16 [768, 768], P(None, 'head'), may hold values from -0.21875 to 0.21875
- w_key: bfloat16 [768, 768], P(None, 'head'), may hold values from -0.21875 to 0.21875
- w_obsval: bfloat16 [768, 768], P(None, 'head'), may hold values from -0.21875 to 0.21875
- w_gridout: bfloat16 [768, 768], P('head'), may hold values from -0.21875 to 0.21875
- w_obsout: bfloat16 [768, 768], P('head'), may hold values from -0.21875 to 0.21875
- obs_count: int32 [128], P('tile'), may hold values from 1 to 2, as said below
- home_block: int32 [256], P('tile'), may hold values from 0 to 1
- seam_block: int32 [256], P('tile'), may hold values from 0 to 3, as said below
Outputs:
- grid_out: bfloat16 [65536, 768], P(('tile', 'head'))
- obs_out: bfloat16 [65536, 768], P(('tile', 'head'))
The draws below stay inside these ranges and needn't reach their ends.
Inputs may be any that keep to these rules, and one draw needn't show every extreme that they name: `obs_count`: every tile has at least one live slot; some tile has all 2 slots live in every draw. `seam_block`: slot 0 of every tile pairs with a block of the previous tile and slot 1 with a block of the next tile; other slots either way.
All inputs are finite; a program needn't handle non-finite values.
Results may differ from the reference program's by a relative error of at most 0.018.
The reference program's roundings to bfloat16 on the way (of `grid_mix` and `obs_mix`) count: a program that leaves them out, or rounds other values in their place, can miss the bound.
Values may be sent and summed in bfloat16 or wider, within the bound.
No kernel may reach another device: no remote copies, remote signals or barrier semaphores. Data moves between devices by JAX's collectives and lax.ppermute only.
A program may use at most 64 MiB of HBM per device.

```python
import jax
import jax.numpy as jnp
from jax import lax

D = 768
HEADS = 12
HD = 64
BS = 256
GB = 2
OB_MAX = 2
TILES = 128
GRID = 65536
OBS = 65536
N_HEAD = 4


def token_draw(key, rows, spread):
    first, second = jax.random.split(key)
    values = jax.random.normal(first, (rows, D), jnp.float32)
    scales = jnp.exp(jax.random.uniform(second, (rows, 1), jnp.float32, 0.0, spread))
    return jnp.clip(values, -6.0, 6.0) * scales


def draw_grid_tokens(key, part):
    key = jax.random.fold_in(key, 11)
    return token_draw(key, GRID, 0.0).astype(jnp.bfloat16)


def draw_obs_tokens(key, part):
    key = jax.random.fold_in(key, 23)
    return token_draw(key, OBS, 0.0).astype(jnp.bfloat16)


def draw_obs_count(key, part):
    key = jax.random.fold_in(key, 37)
    first, second = jax.random.split(key)
    counts = jax.random.randint(first, (TILES,), 1, OB_MAX + 1)
    busiest = jax.random.randint(second, (), 0, TILES)
    counts = jnp.where(jnp.arange(TILES) == busiest, OB_MAX, counts)
    return counts.astype(jnp.int32)


def draw_seam_block(key, part):
    key = jax.random.fold_in(key, 53)
    raw = jax.random.randint(key, (TILES * OB_MAX,), 0, 2 * GB)
    position = jnp.arange(TILES * OB_MAX) % OB_MAX
    values = jnp.where(position == 0, raw % GB, jnp.where(position == 1, GB + raw % GB, raw))
    return values.astype(jnp.int32)


def touch_ends(values, key, smallest, high):
    index_at = [jax.random.randint(jax.random.fold_in(key, axis), (), 0, length) for axis, length in enumerate(values.shape)]
    longest = values.shape.index(max(values.shape))
    beside = index_at[:longest] + [(index_at[longest] + 1) % values.shape[longest]] + index_at[longest + 1:]
    return values.at[tuple(index_at)].set(smallest).at[tuple(beside)].set(high)


def block_levels(key, dims, cuts, low, high):
    def one(dim, parts):
        heights = jax.random.uniform(jax.random.fold_in(jax.random.fold_in(key, 6), dim), (parts,), jnp.float32, low / len(cuts), high / len(cuts))
        return jnp.repeat(jnp.exp(heights), dims[dim] // parts).reshape((-1,) + (1,) * (len(dims) - dim - 1))

    loudness = one(*cuts[0])
    for cut in cuts[1:]:
        loudness = loudness * one(*cut)
    return loudness


def normal_values(own_key, dims, scale, reach, cuts=(), kind=jnp.bfloat16):
    loudness = block_levels(own_key, dims, cuts, -0.22, 0.18) if cuts else 1.0
    result = jax.random.normal(own_key, dims, jnp.float32) * scale * loudness
    return jnp.minimum(jnp.maximum(result, -reach), reach).astype(kind)


def setup_inputs(seed: int = 0) -> dict:
    splits = jax.random.split(jax.random.key(seed), 12)
    grid_tokens = draw_grid_tokens(jax.random.fold_in(splits[11], 71), 0)
    obs_tokens = draw_obs_tokens(jax.random.fold_in(splits[11], 71), 0)
    w_query = normal_values(splits[2], (D, D), D ** -0.5, 0.21875, ((1, 4),))
    w_gridval = normal_values(splits[3], (D, D), D ** -0.5, 0.21875, ((1, 4),))
    w_key = normal_values(splits[4], (D, D), D ** -0.5, 0.21875, ((1, 4),))
    w_obsval = normal_values(splits[5], (D, D), D ** -0.5, 0.21875, ((1, 4),))
    w_gridout = normal_values(splits[6], (D, D), D ** -0.5, 0.21875, ((0, 4),))
    w_obsout = normal_values(splits[7], (D, D), D ** -0.5, 0.21875, ((0, 4),))
    obs_count = draw_obs_count(jax.random.fold_in(splits[11], 71), 0)
    home_block = touch_ends(jax.random.randint(splits[9], (TILES * OB_MAX,), 0, GB), jax.random.fold_in(splits[9], 1), 0, GB - 1).astype(jnp.int32)
    seam_block = draw_seam_block(jax.random.fold_in(splits[11], 71), 0)
    return {"grid_tokens": grid_tokens, "obs_tokens": obs_tokens, "w_query": w_query, "w_gridval": w_gridval, "w_key": w_key, "w_obsval": w_obsval, "w_gridout": w_gridout, "w_obsout": w_obsout, "obs_count": obs_count, "home_block": home_block, "seam_block": seam_block}


NEG = -1e30


def pair_stats(q, k, vgrid, vobs):
    s = jnp.einsum('ihd,jhd->hij', q.astype(jnp.float32), k.astype(jnp.float32)) / (HD ** 0.5)
    mg = jnp.max(s, axis=2)
    eg = jnp.exp(s - mg[:, :, None]).astype(jnp.bfloat16)
    lg = jnp.sum(eg.astype(jnp.float32), axis=2)
    ag = jnp.einsum('hij,jhd->ihd', eg.astype(jnp.float32), vobs.astype(jnp.float32))
    mo = jnp.max(s, axis=1)
    eo = jnp.exp(s - mo[:, None, :]).astype(jnp.bfloat16)
    lo = jnp.sum(eo.astype(jnp.float32), axis=1)
    ao = jnp.einsum('hij,ihd->jhd', eo.astype(jnp.float32), vgrid.astype(jnp.float32))
    return mg, lg, ag, mo, lo, ao


def project(mix, weight):
    width = D // N_HEAD
    total = jnp.zeros((mix.shape[0], D), jnp.float32)
    for k in range(N_HEAD):
        part = jnp.dot(mix[:, k * width:(k + 1) * width], weight[k * width:(k + 1) * width], preferred_element_type=jnp.float32)
        total = total + part.astype(jnp.bfloat16).astype(jnp.float32)
    return total.astype(jnp.bfloat16)


def reference(grid_tokens, obs_tokens, w_query, w_gridval, w_key, w_obsval, w_gridout, w_obsout, obs_count, home_block, seam_block):
    query = jnp.dot(grid_tokens, w_query, preferred_element_type=jnp.float32).astype(jnp.bfloat16).reshape(TILES * GB, BS, HEADS, HD)
    grid_value = jnp.dot(grid_tokens, w_gridval, preferred_element_type=jnp.float32).astype(jnp.bfloat16).reshape(TILES * GB, BS, HEADS, HD)
    key = jnp.dot(obs_tokens, w_key, preferred_element_type=jnp.float32).astype(jnp.bfloat16).reshape(TILES * OB_MAX, BS, HEADS, HD)
    obs_value = jnp.dot(obs_tokens, w_obsval, preferred_element_type=jnp.float32).astype(jnp.bfloat16).reshape(TILES * OB_MAX, BS, HEADS, HD)
    slots = jnp.arange(TILES * OB_MAX, dtype=jnp.int32)
    tile_of = slots // OB_MAX
    live = (slots % OB_MAX) < obs_count[tile_of]
    home_global = tile_of * GB + home_block
    seam_tile = jnp.where(seam_block < GB, tile_of - 1, tile_of + 1) % TILES
    seam_global = (seam_tile * GB + seam_block % GB).astype(jnp.int32)
    targets = jnp.concatenate([home_global, seam_global]).astype(jnp.int32)
    sources = jnp.concatenate([slots, slots]).astype(jnp.int32)
    live_pair = jnp.concatenate([live, live])

    def one(idx):
        g, o = idx
        return pair_stats(query[g], key[o], grid_value[g], obs_value[o])

    mg, lg, ag, mo, lo, ao = lax.map(one, (targets, sources))
    count = TILES * OB_MAX
    m_obs = jnp.maximum(mo[:count], mo[count:])
    w_home = jnp.exp(mo[:count] - m_obs)
    w_seam = jnp.exp(mo[count:] - m_obs)
    l_obs = w_home * lo[:count] + w_seam * lo[count:]
    a_obs = jnp.transpose(w_home, (0, 2, 1))[..., None] * ao[:count] + jnp.transpose(w_seam, (0, 2, 1))[..., None] * ao[count:]
    obs_mix = a_obs / jnp.transpose(l_obs, (0, 2, 1))[..., None]
    obs_mix = jnp.where(live[:, None, None, None], obs_mix, 0.0).astype(jnp.bfloat16).reshape(OBS, D)

    mg_live = jnp.where(live_pair[:, None, None], mg, NEG)
    m_blk = jnp.full((TILES * GB, HEADS, BS), NEG, jnp.float32).at[targets].max(mg_live)
    weight = jnp.where(live_pair[:, None, None], jnp.exp(mg_live - m_blk[targets]), 0.0)
    l_blk = jnp.zeros((TILES * GB, HEADS, BS), jnp.float32).at[targets].add(weight * lg)
    a_blk = jnp.zeros((TILES * GB, BS, HEADS, HD), jnp.float32).at[targets].add(jnp.transpose(weight, (0, 2, 1))[..., None] * ag)
    l_safe = jnp.where(l_blk > 0, l_blk, 1.0)
    grid_mix = (a_blk / jnp.transpose(l_safe, (0, 2, 1))[..., None]).astype(jnp.bfloat16).reshape(GRID, D)
    return project(grid_mix, w_gridout), project(obs_mix, w_obsout)
```

```python
import jax
import jax.numpy as jnp
from jax import lax
from jax.experimental import pallas as pl
from jax.experimental.pallas import tpu as pltpu
from jax.sharding import PartitionSpec as P

HD = 64
BS = 256
HEADS = 3
WIDTH = HEADS * HD
GROUPS = 4
D = 768
NEG = -1e30
PAY = 3 * BS + 16
NT = (((1,), (1,)), ((), ()))
VMEM_LIMIT = 48 * 1024 * 1024


def dot32(a, b):
    return jnp.dot(a, b, preferred_element_type=jnp.float32)


def lanes(width):
    return lax.broadcasted_iota(jnp.int32, (1, width), 1)


def project_kernel(par, count, seam, grid, obs, w_q, w_gv, w_k, w_ov, pay_a, pay_b):
    slot_b = par[0]
    x = jnp.concatenate(
        [dot32(grid[...], w_q[...]).astype(jnp.bfloat16), dot32(grid[...], w_gv[...]).astype(jnp.bfloat16)], axis=1
    )
    pay_a[: 2 * BS] = x
    pay_b[: 2 * BS] = x
    for pay, slot in ((pay_a, 1 - slot_b), (pay_b, slot_b)):
        rows = obs[pl.ds(pl.multiple_of(slot * BS, BS), BS)]
        pay[2 * BS : 3 * BS] = jnp.concatenate(
            [dot32(rows, w_k[...]).astype(jnp.bfloat16), dot32(rows, w_ov[...]).astype(jnp.bfloat16)], axis=1
        )
        target = (seam[slot] & 1).astype(jnp.float32)
        live = (slot < count[0]).astype(jnp.float32)
        flags = jnp.where(lax.broadcasted_iota(jnp.int32, (16, 2 * WIDTH), 1) < 128, target, live)
        pay[3 * BS :] = flags.astype(jnp.bfloat16)


def side(x, y):
    lane = lanes(BS)
    left = x[:, :BS]
    right = y[:, :BS]
    vals = jnp.where(lane < HD, jnp.bfloat16(1.0), y[:, 2 * HD :])
    out = total = top = None
    for h in range(HEADS):
        pick = jnp.where((lane >= h * HD) & (lane < (h + 1) * HD), 0.125, 0.0).astype(jnp.bfloat16)
        s = lax.dot_general(left * pick, right, NT, preferred_element_type=jnp.float32)
        m = jnp.max(s, axis=1, keepdims=True)
        e = jnp.exp(s - m).astype(jnp.bfloat16)
        o = dot32(e, vals)
        l = o[:, :1]
        if h == 0:
            out, total, top = o, jnp.broadcast_to(l, o.shape), jnp.broadcast_to(m, o.shape)
        else:
            mine = lane >= (h + 1) * HD
            out = jnp.where(mine, o, out)
            total = jnp.where(mine, l, total)
            top = jnp.where(mine, m, top)
    return out, total, top


def merge(first, second):
    top = jnp.maximum(first[2], second[2])
    w1 = jnp.exp(first[2] - top)
    w2 = jnp.exp(second[2] - top)
    return w1 * first[0] + w2 * second[0], w1 * first[1] + w2 * second[1], top


def attend_kernel(par, count, home, seam, pay_a, pay_b, rec_a, rec_b, out, acc, mix):
    slot_b = par[0]
    acc[:, 0] = jnp.zeros_like(acc[:, 0])
    acc[:, 1] = jnp.zeros_like(acc[:, 1])
    acc[:, 2] = jnp.full_like(acc[:, 2], NEG)
    mix[...] = jnp.zeros_like(mix)

    def add(block, part):
        now = merge((acc[block, 0], acc[block, 1], acc[block, 2]), part)
        for i in range(3):
            acc[block, i] = now[i]

    for slot, pay, rec in ((1 - slot_b, pay_a, rec_a), (slot_b, pay_b, rec_b)):

        @pl.when(slot < count[0])
        def _():
            kv = pay[2 * BS : 3 * BS]
            block = home[slot]
            x = pay[pl.ds(pl.multiple_of(block * BS, BS), BS)]
            add(block, side(x, kv))
            x2 = rec[pl.ds(pl.multiple_of((seam[slot] & 1) * BS, BS), BS)]
            o, l, _m = merge(side(kv, x), side(kv, x2))
            mix[2 + slot] = (o / l).astype(jnp.bfloat16)

        flags = rec[3 * BS :, :BS].astype(jnp.float32)
        block_in = jnp.max(flags[:, :128]).astype(jnp.int32)
        live_in = jnp.max(flags[:, 128:]) > 0.5

        @pl.when(live_in)
        def _():
            kv = rec[2 * BS : 3 * BS]
            x = pay[pl.ds(pl.multiple_of(block_in * BS, BS), BS)]
            add(block_in, side(x, kv))

    for block in range(2):
        l = acc[block, 1]
        mix[block] = (acc[block, 0] / jnp.where(l > 0, l, 1.0)).astype(jnp.bfloat16)
    for block in range(2):
        g = mix[block]
        o = mix[2 + block]
        first = jnp.where(lanes(128) < HD, pltpu.roll(o[:, :128], HD, 1), g[:, :128])
        whole = jnp.concatenate([first, g[:, 128:], o[:, 128:]], axis=1)
        out[2 * block] = whole[:128]
        out[2 * block + 1] = whole[128:]


def out_kernel(par, mixes, w_own, w_other, grid_out, obs_out):
    def apply(part, w):
        total = None
        for k in range(GROUPS):
            rows = mixes[k]
            if part == 0:
                rows = rows[:, HD : HD + WIDTH]
            else:
                rows = jnp.concatenate([rows[:, :HD], rows[:, HD + WIDTH :]], axis=1)
            piece = dot32(rows, w[k]).astype(jnp.bfloat16).astype(jnp.float32)
            total = piece if total is None else total + piece
        return total.astype(jnp.bfloat16)

    @pl.when(par[0] == 0)
    def _():
        grid_out[...] = apply(0, w_own)
        obs_out[...] = apply(1, w_other)

    @pl.when(par[0] == 1)
    def _():
        grid_out[...] = apply(0, w_other)
        obs_out[...] = apply(1, w_own)


SMEM = pl.BlockSpec(memory_space=pltpu.SMEM)
VMEM = pl.BlockSpec(memory_space=pltpu.VMEM)
PARAMS = pltpu.CompilerParams(vmem_limit_bytes=VMEM_LIMIT)


def body(
    grid_tokens, obs_tokens, w_query, w_gridval, w_key, w_obsval, w_gridout, w_obsout, obs_count, home_block, seam_block
):
    tiles = lax.axis_size("tile")
    parity = lax.axis_index("tile").astype(jnp.int32) % 2
    par = parity.reshape(1)
    swap_a = [(i, i ^ 1) for i in range(tiles)]
    swap_b = [(i, (i + 1) % tiles if i % 2 else (i - 1) % tiles) for i in range(tiles)]
    pay_shape = jax.ShapeDtypeStruct((PAY, 2 * WIDTH), jnp.bfloat16)
    pay_a, pay_b = pl.pallas_call(
        project_kernel,
        out_shape=(pay_shape, pay_shape),
        in_specs=[SMEM] * 3 + [VMEM] * 6,
        out_specs=(VMEM, VMEM),
        compiler_params=PARAMS,
        cost_estimate=pl.CostEstimate(flops=604_000_000, bytes_accessed=4_000_000, transcendentals=0),
    )(par, obs_count, seam_block, grid_tokens, obs_tokens, w_query, w_gridval, w_key, w_obsval)
    rec_b = lax.ppermute(pay_b, "tile", swap_b)
    rec_a = lax.ppermute(pay_a, "tile", swap_a)
    w_mine = jnp.where(parity == 0, w_gridout, w_obsout)
    w_own = lax.all_to_all(
        jnp.broadcast_to(w_mine[None], (GROUPS,) + w_mine.shape), "head", split_axis=0, concat_axis=0, tiled=True
    )
    w_other = lax.ppermute(w_own, "tile", swap_a)
    mix = pl.pallas_call(
        attend_kernel,
        out_shape=jax.ShapeDtypeStruct((GROUPS, 128, 2 * WIDTH), jnp.bfloat16),
        in_specs=[SMEM] * 4 + [VMEM] * 4,
        out_specs=VMEM,
        scratch_shapes=[pltpu.VMEM((2, 3, BS, BS), jnp.float32), pltpu.VMEM((4, BS, BS), jnp.bfloat16)],
        compiler_params=PARAMS,
        cost_estimate=pl.CostEstimate(flops=1_200_000_000, bytes_accessed=2_400_000, transcendentals=1_600_000),
    )(par, obs_count, home_block, seam_block, pay_a, pay_b, rec_a, rec_b)
    mixes = lax.all_to_all(mix, "head", split_axis=0, concat_axis=0, tiled=True)
    out_shape = jax.ShapeDtypeStruct((128, D), jnp.bfloat16)
    return pl.pallas_call(
        out_kernel,
        out_shape=(out_shape, out_shape),
        in_specs=[SMEM] + [VMEM] * 3,
        out_specs=(VMEM, VMEM),
        compiler_params=PARAMS,
        cost_estimate=pl.CostEstimate(flops=302_000_000, bytes_accessed=3_000_000, transcendentals=0),
    )(par, mixes, w_own, w_other)


def solution(mesh):
    return jax.shard_map(
        body,
        mesh=mesh,
        in_specs=(
            P("tile", None),
            P("tile", None),
            P(None, "head"),
            P(None, "head"),
            P(None, "head"),
            P(None, "head"),
            P("head", None),
            P("head", None),
            P("tile"),
            P("tile"),
            P("tile"),
        ),
        out_specs=(P(("tile", "head"), None), P(("tile", "head"), None)),
        check_vma=False,
    )
```

```python
import jax
import jax.numpy as jnp
from jax import lax
from jax.experimental import pallas as pl
from jax.experimental.pallas import tpu as pltpu
from jax.sharding import PartitionSpec as P

HD = 64
BS = 256
HEADS = 3
WIDTH = HEADS * HD
PAIR = 2 * WIDTH
GROUPS = 4
D = 768
NEG = -1e30
ROWS_O = HD + 16
PAY = 3 * PAIR + 16
NT = (((1,), (1,)), ((), ()))
TN = (((0,), (0,)), ((), ()))
VMEM_LIMIT = 48 * 1024 * 1024


def dot32(a, b):
    return jnp.dot(a, b, preferred_element_type=jnp.float32)


def parity():
    return lax.axis_index("tile") % 2


def slots():
    return 1 - parity(), parity()


def write_flags(pay, slot, count, seam):
    target = (seam[slot] & 1).astype(jnp.float32)
    live = (slot < count[0]).astype(jnp.float32)
    flags = jnp.where(lax.broadcasted_iota(jnp.int32, (16, BS), 1) < 128, target, live)
    pay[3 * PAIR :] = flags.astype(jnp.bfloat16)


def project_kernel(
    count, seam_hbm, grid, obs, w_q, w_gv, w_k, w_ov, w_g, w_o, pay_a, pay_b, spread, tok, wts, seam, sems, sem_w
):
    slot_a, slot_b = slots()

    def rows(ref, block):
        return ref.at[pl.ds(pl.multiple_of(block * BS, BS), BS)]

    weights = (w_q, w_gv, w_k, w_ov)
    load_w = [pltpu.make_async_copy(w, wts.at[pl.ds(i * WIDTH, WIDTH)], sems.at[i]) for i, w in enumerate(weights)]
    load_g = pltpu.make_async_copy(grid, tok.at[pl.ds(0, 2 * BS)], sems.at[4])
    load_b = pltpu.make_async_copy(rows(obs, slot_b), tok.at[pl.ds(2 * BS, BS)], sems.at[5])
    load_a = pltpu.make_async_copy(rows(obs, slot_a), tok.at[pl.ds(3 * BS, BS)], sems.at[6])
    load_seam = pltpu.make_async_copy(seam_hbm, seam, sems.at[7])
    for copy in (load_w[0], load_w[1], load_g, load_w[2], load_w[3], load_b, load_a, load_seam):
        copy.start()

    def send(ref, start):
        for k in range(GROUPS):
            copy = pltpu.make_async_copy(ref, spread.at[k], sem_w.at[k])
            copy.start() if start else copy.wait()

    @pl.when(slot_b == 0)
    def _():
        send(w_g, True)

    @pl.when(slot_b == 1)
    def _():
        send(w_o, True)

    def project(i):
        w = wts[i * PAIR : (i + 1) * PAIR]
        t = tok[2 * i * BS : 2 * (i + 1) * BS]
        return lax.dot_general(w, t, NT, preferred_element_type=jnp.float32).astype(jnp.bfloat16)

    load_w[0].wait()
    load_w[1].wait()
    load_g.wait()
    x = project(0)
    for block in range(2):
        part = x[:, block * BS : (block + 1) * BS]
        pay_a[block * PAIR : (block + 1) * PAIR] = part
        pay_b[block * PAIR : (block + 1) * PAIR] = part
    load_w[2].wait()
    load_w[3].wait()
    load_b.wait()
    load_a.wait()
    x = project(1)
    pay_b[2 * PAIR : 3 * PAIR] = x[:, :BS]
    pay_a[2 * PAIR : 3 * PAIR] = x[:, BS:]
    load_seam.wait()
    write_flags(pay_a, slot_a, count, seam)
    write_flags(pay_b, slot_b, count, seam)
    send(w_g, False)


def row_major(x_t):
    return jnp.transpose(x_t) * jnp.bfloat16(0.125)


def side(left, right_t, vals_t):
    lane = lax.broadcasted_iota(jnp.int32, (1, WIDTH), 1)
    ones = jnp.ones((ROWS_O - HD, BS), jnp.bfloat16)
    parts = []
    for h in range(HEADS):
        mine = (lane >= h * HD) & (lane < (h + 1) * HD)
        s = dot32(jnp.where(mine, left, jnp.bfloat16(0.0)), right_t)
        m = jnp.max(s, axis=0, keepdims=True)
        e = jnp.exp(s - m).astype(jnp.bfloat16)
        parts.append((dot32(jnp.concatenate([vals_t[h * HD : (h + 1) * HD], ones], axis=0), e), m))
    return parts


def fold(acc, top, index, parts):
    for h, (o, m) in enumerate(parts):
        old = top[index, h, :1]
        new = jnp.maximum(old, m)
        acc[index, h] = acc[index, h] * jnp.exp(old - new) + o * jnp.exp(m - new)
        top[index, h] = jnp.broadcast_to(new, (8, BS))


def put(acc, top, index, parts):
    for h, (o, m) in enumerate(parts):
        acc[index, h] = o
        top[index, h] = jnp.broadcast_to(m, (8, BS))


def block_rows(ref, block):
    start = pl.multiple_of(block * PAIR, WIDTH)
    return ref[pl.ds(start, WIDTH)], ref[pl.ds(pl.multiple_of(start + WIDTH, WIDTH), WIDTH)]


def home_kernel(count, home, pay_a, pay_b, acc, top):
    acc[...] = jnp.zeros_like(acc)
    top[...] = jnp.full_like(top, NEG)
    for i, (slot, pay) in enumerate(zip(slots(), (pay_a, pay_b))):

        @pl.when(slot < count[0])
        def _():
            block = home[slot]
            q_t, gv_t = block_rows(pay, block)
            k_t, ov_t = block_rows(pay, 2)
            fold(acc, top, block, side(row_major(k_t), q_t, ov_t))
            put(acc, top, 2 + i, side(row_major(q_t), k_t, gv_t))


def seam_step(i, count, seam, pay, rec, acc, top):
    slot = slots()[i]
    flags = rec[3 * PAIR :].astype(jnp.float32)
    block_in = jnp.max(flags[:, :128]).astype(jnp.int32)
    live_in = jnp.max(flags[:, 128:]) > 0.5

    @pl.when(live_in)
    def _():
        q_t, _gv = block_rows(pay, block_in)
        k_t, ov_t = block_rows(rec, 2)
        fold(acc, top, block_in, side(row_major(k_t), q_t, ov_t))

    @pl.when(slot < count[0])
    def _():
        q_t, gv_t = block_rows(rec, seam[slot] & 1)
        k_t, _ov = block_rows(pay, 2)
        fold(acc, top, 2 + i, side(row_major(q_t), k_t, gv_t))


def near_kernel(count, seam, pay, rec, _acc, _top, acc, top):
    seam_step(0, count, seam, pay, rec, acc, top)


def far_kernel(count, seam, pay, rec, _acc, _top, *refs):
    outs, (acc, top, mix) = refs[:-3], refs[-3:]
    seam_step(1, count, seam, pay, rec, acc, top)
    if len(outs) == 1:
        mix = outs[0]
    slot_a, slot_b = slots()
    for index in range(4):
        if index < 2:
            chunk, first = 2 * index, 0
        else:
            chunk, first = 2 * (slot_a if index == 2 else slot_b), WIDTH
        for h in range(HEADS):
            o = acc[index, h]
            l = o[HD : HD + 1]
            value = (o[:HD] / jnp.where(l > 0, l, 1.0)).astype(jnp.bfloat16)
            at = first + h * HD
            mix[chunk, at : at + HD] = value[:, :128]
            mix[chunk + 1, at : at + HD] = value[:, 128:]
    if len(outs) > 1:
        for s, out in enumerate(outs):
            out[...] = mix[(lax.axis_index("head") + s) % GROUPS]


def out_kernel(*refs):
    mixes, (w_own, w_other, grid_out, obs_out) = refs[:-4], refs[-4:]

    def apply(part, w):
        total = None
        for s in range(GROUPS):
            if len(mixes) == 1:
                k, mix = s, mixes[0].at[s]
            else:
                k, mix = (lax.axis_index("head") + GROUPS - s) % GROUPS, mixes[s]
            rows = mix[part * WIDTH : (part + 1) * WIDTH]
            piece = lax.dot_general(rows, w[k], TN, preferred_element_type=jnp.float32)
            piece = piece.astype(jnp.bfloat16).astype(jnp.float32)
            total = piece if total is None else total + piece
        return total.astype(jnp.bfloat16)

    @pl.when(parity() == 0)
    def _():
        grid_out[...] = apply(0, w_own)
        obs_out[...] = apply(1, w_other)

    @pl.when(parity() == 1)
    def _():
        grid_out[...] = apply(0, w_other)
        obs_out[...] = apply(1, w_own)


SMEM = pl.BlockSpec(memory_space=pltpu.SMEM)
VMEM = pl.BlockSpec(memory_space=pltpu.VMEM)
ANY = pl.BlockSpec(memory_space=pltpu.HBM)
PARAMS = pltpu.CompilerParams(vmem_limit_bytes=VMEM_LIMIT)


def in_hbm(x):
    return pltpu.with_memory_space_constraint(x, pltpu.HBM)


def in_vmem(x):
    return pltpu.with_memory_space_constraint(x, pltpu.VMEM)


def cost(flops, moved, exps=0):
    return pl.CostEstimate(flops=flops, bytes_accessed=moved, transcendentals=exps)


MIX_BY_PERMUTE = False


def body(
    grid_tokens, obs_tokens, w_query, w_gridval, w_key, w_obsval, w_gridout, w_obsout, obs_count, home_block, seam_block
):
    tiles = lax.axis_size("tile")
    swap_a = [(i, i ^ 1) for i in range(tiles)]
    swap_b = [(i, (i + 1) % tiles if i % 2 else (i - 1) % tiles) for i in range(tiles)]
    f32, bf16 = jnp.float32, jnp.bfloat16
    pay_shape = pltpu.VMEM((PAY, BS), bf16)
    acc_shape = pltpu.VMEM((4, HEADS, ROWS_O, BS), f32)
    top_shape = pltpu.VMEM((4, HEADS, 8, BS), f32)
    mix_shape = jax.ShapeDtypeStruct((PAIR, 128), bf16)
    mixes_shape = pltpu.VMEM((GROUPS, PAIR, 128), bf16)
    w_shape = pltpu.VMEM((GROUPS, WIDTH, D), bf16)
    out_shape = jax.ShapeDtypeStruct((128, D), bf16)

    pay_a, pay_b, w_spread = pl.pallas_call(
        project_kernel,
        out_shape=(pay_shape, pay_shape, w_shape),
        in_specs=[SMEM] + [ANY] * 9,
        out_specs=(VMEM, VMEM, VMEM),
        scratch_shapes=[
            pltpu.VMEM((4 * BS, D), bf16),
            pltpu.VMEM((4 * WIDTH, D), bf16),
            pltpu.SMEM((2,), jnp.int32),
            pltpu.SemaphoreType.DMA((8,)),
            pltpu.SemaphoreType.DMA((GROUPS,)),
        ],
        compiler_params=PARAMS,
        cost_estimate=cost(1, 1),
    )(
        obs_count,
        *map(
            in_hbm,
            (seam_block, grid_tokens, obs_tokens, w_query.T, w_gridval.T, w_key.T, w_obsval.T, w_gridout, w_obsout),
        ),
    )
    w_own = lax.all_to_all(w_spread, "head", split_axis=0, concat_axis=0, tiled=True)
    rec_b = lax.ppermute(pay_b, "tile", swap_b)
    acc, top = pl.pallas_call(
        home_kernel,
        out_shape=(acc_shape, top_shape),
        in_specs=[SMEM] * 2 + [VMEM] * 2,
        out_specs=(VMEM, VMEM),
        compiler_params=PARAMS,
        cost_estimate=cost(10**10, 1),
    )(obs_count, home_block, pay_a, pay_b)
    pay_a2 = pay_a
    rec_a = lax.ppermute(pay_a2, "tile", swap_a)
    acc, top = pl.pallas_call(
        near_kernel,
        out_shape=(acc_shape, top_shape),
        in_specs=[SMEM] * 2 + [VMEM] * 4,
        out_specs=(VMEM, VMEM),
        input_output_aliases={4: 0, 5: 1},
        compiler_params=PARAMS,
        cost_estimate=cost(1, 1),
    )(obs_count, seam_block, pay_a, in_vmem(rec_a), acc, top)
    count = GROUPS if MIX_BY_PERMUTE else 1
    mixes = pl.pallas_call(
        far_kernel,
        out_shape=((mix_shape,) * GROUPS if MIX_BY_PERMUTE else (mixes_shape,)) + (acc_shape, top_shape),
        in_specs=[SMEM] * 2 + [VMEM] * 4,
        out_specs=(VMEM,) * (count + 2),
        input_output_aliases={4: count, 5: count + 1},
        scratch_shapes=[pltpu.VMEM(mixes_shape.shape if MIX_BY_PERMUTE else (1, 16, 128), bf16)],
        compiler_params=PARAMS,
        cost_estimate=cost(1, 1),
    )(obs_count, seam_block, pay_b, in_vmem(rec_b), acc, top)
    late = mixes[0]
    if MIX_BY_PERMUTE:
        mixes = [mixes[0]] + [
            lax.ppermute(mixes[s], "head", [(i, (i + s) % GROUPS) for i in range(GROUPS)]) for s in (1, 2, 3)
        ]
    else:
        mixes = [lax.all_to_all(mixes[0], "head", split_axis=0, concat_axis=0, tiled=True)]
    w_own2, _ = lax.optimization_barrier((w_own, rec_a))
    w_other = lax.ppermute(w_own2, "tile", swap_a)
    return pl.pallas_call(
        out_kernel,
        out_shape=(out_shape, out_shape),
        in_specs=[VMEM] * (count + 2),
        out_specs=(VMEM, VMEM),
        compiler_params=PARAMS,
        cost_estimate=cost(1, 1),
    )(*map(in_vmem, mixes), in_vmem(w_own), in_vmem(w_other))


def solution(mesh):
    return jax.shard_map(
        body,
        mesh=mesh,
        in_specs=(
            P("tile", None),
            P("tile", None),
            P(None, "head"),
            P(None, "head"),
            P(None, "head"),
            P(None, "head"),
            P("head", None),
            P("head", None),
            P("tile"),
            P("tile"),
            P("tile"),
        ),
        out_specs=(P(("tile", "head"), None), P(("tile", "head"), None)),
        check_vma=False,
    )
```

```python
import jax
import jax.numpy as jnp
from jax import lax
from jax.experimental import pallas as pl
from jax.experimental.pallas import tpu as pltpu
from jax.sharding import PartitionSpec as P

HD = 64
BS = 256
HEADS = 3
WIDTH = HEADS * HD
PAIR = 2 * WIDTH
GROUPS = 4
D = 768
NEG = -1e30
ROWS_O = HD + 16
PAY = 3 * PAIR + 16
PAY_B = PAY + 64
NT = (((1,), (1,)), ((), ()))
TN = (((0,), (0,)), ((), ()))
VMEM_LIMIT = 48 * 1024 * 1024


def dot32(a, b):
    return jnp.dot(a, b, preferred_element_type=jnp.float32)


def parity():
    return lax.axis_index("tile") % 2


def slots():
    return 1 - parity(), parity()


def write_flags(pay, slot, count, home, seam):
    lane = lax.broadcasted_iota(jnp.int32, (16, BS), 1)
    live = (slot < count[0]).astype(jnp.int32)
    flags = jnp.where(lane < 64, seam[slot] & 1, jnp.where(lane < 128, live, home[slot]))
    pay[3 * PAIR : PAY] = flags.astype(jnp.float32).astype(jnp.bfloat16)


def read_flags(pay):
    flags = pay[3 * PAIR : PAY].astype(jnp.float32)
    target, live, home = (jnp.max(flags[:, 64 * i : 64 * (i + 1)]).astype(jnp.int32) for i in range(3))
    return target, live > 0, home


def project_kernel(
    count_any, home_hbm, seam_hbm, grid, obs, w_q, w_gv, w_k, w_ov, w_g, w_o, pay_a, pay_b, spread, tok, wts, seam, home, count, sems
):
    slot_a, slot_b = slots()

    def rows(ref, block):
        return ref.at[pl.ds(pl.multiple_of(block * BS, BS), BS)]

    weights = (w_q, w_gv, w_k, w_ov)
    load_w = [pltpu.make_async_copy(w, wts.at[pl.ds(i * WIDTH, WIDTH)], sems.at[i]) for i, w in enumerate(weights)]
    load_g = pltpu.make_async_copy(grid, tok.at[pl.ds(0, 2 * BS)], sems.at[4])
    load_b = pltpu.make_async_copy(rows(obs, slot_b), tok.at[pl.ds(2 * BS, BS)], sems.at[5])
    load_a = pltpu.make_async_copy(rows(obs, slot_a), tok.at[pl.ds(3 * BS, BS)], sems.at[6])
    load_seam = pltpu.make_async_copy(seam_hbm, seam, sems.at[7])
    load_home = pltpu.make_async_copy(home_hbm, home, sems.at[10])
    load_count = pltpu.make_async_copy(count_any, count, sems.at[8])
    for copy in (load_w[0], load_w[1], load_g, load_w[2], load_w[3], load_b, load_a, load_seam, load_home, load_count):
        copy.start()

    load_s = [pltpu.make_async_copy(w, spread.at[0], sems.at[9]) for w in (w_g, w_o)]

    @pl.when(slot_b == 0)
    def _():
        load_s[0].start()

    @pl.when(slot_b == 1)
    def _():
        load_s[1].start()

    def project(i):
        w = wts[i * PAIR : (i + 1) * PAIR]
        t = tok[2 * i * BS : 2 * (i + 1) * BS]
        return lax.dot_general(w, t, NT, preferred_element_type=jnp.float32).astype(jnp.bfloat16)

    load_seam.wait()
    load_home.wait()
    load_count.wait()
    write_flags(pay_a, slot_a, count, home, seam)
    write_flags(pay_b, slot_b, count, home, seam)
    load_w[0].wait()
    load_w[1].wait()
    load_g.wait()
    x = project(0)
    for block in range(2):
        part = x[:, block * BS : (block + 1) * BS]
        pay_a[block * PAIR : (block + 1) * PAIR] = part
        pay_b[block * PAIR : (block + 1) * PAIR] = part
    load_w[2].wait()
    load_w[3].wait()
    load_b.wait()
    load_a.wait()
    x = project(1)
    pay_b[2 * PAIR : 3 * PAIR] = x[:, :BS]
    pay_a[2 * PAIR : 3 * PAIR] = x[:, BS:]
    load_s[0].wait()
    for k in range(1, GROUPS):
        spread[k] = spread[0]


def attend(tasks):
    ones = jnp.ones((ROWS_O - HD, BS), jnp.bfloat16)
    heads = [slice(h * HD, (h + 1) * HD) for h in range(HEADS)]
    scores = []
    for rows_t, columns_t, _values in tasks:
        for at in heads:
            rows = jnp.transpose(rows_t[at]) * jnp.bfloat16(0.125)
            scores.append(dot32(rows, columns_t[at]))
    parts = []
    for index, s in enumerate(scores):
        values = tasks[index // HEADS][2][heads[index % HEADS]]
        m = jnp.max(s, axis=0, keepdims=True)
        e = jnp.exp(s - m).astype(jnp.bfloat16)
        parts.append((dot32(jnp.concatenate([values, ones], axis=0), e), m))
    return [parts[HEADS * t : HEADS * (t + 1)] for t in range(len(tasks))]


def fold(acc, top, index, parts, live):
    for h, (o, m) in enumerate(parts):
        old = top[index, h, :1]
        new = jnp.where(live, jnp.maximum(old, m), old)
        weight = jnp.where(live, jnp.exp(m - new), 0.0)
        acc[index, h] = acc[index, h] * jnp.exp(old - new) + o * weight
        top[index, h] = jnp.broadcast_to(new, (8, BS))


def block_rows(ref, block):
    start = pl.multiple_of(block * PAIR, WIDTH)
    return ref[pl.ds(start, WIDTH)], ref[pl.ds(pl.multiple_of(start + WIDTH, WIDTH), WIDTH)]


def home_kernel(pay_a, pay_b, acc, top):
    tasks, blocks, lives = [], [], []
    for pay in (pay_a, pay_b):
        _target, live, block = read_flags(pay)
        q_t, gv_t = block_rows(pay, block)
        k_t, ov_t = block_rows(pay, 2)
        tasks += [(k_t, q_t, ov_t), (q_t, k_t, gv_t)]
        blocks.append(block)
        lives.append(live)
    grid_a, obs_a, grid_b, obs_b = attend(tasks)
    for index, parts in ((2, obs_a), (3, obs_b)):
        for h, (o, m) in enumerate(parts):
            acc[index, h] = o
            top[index, h] = jnp.broadcast_to(m, (8, BS))
    for block in range(2):
        used = [(b == block) & live for b, live in zip(blocks, lives)]
        for h in range(HEADS):
            pair = (grid_a[h], grid_b[h])
            new = jnp.maximum(*[jnp.where(u, m, NEG) for u, (_o, m) in zip(used, pair)])
            first, second = [o * jnp.where(u, jnp.exp(m - new), 0.0) for u, (o, m) in zip(used, pair)]
            acc[block, h] = first + second
            top[block, h] = jnp.broadcast_to(new, (8, BS))


def seam_kernel(pay_a, pay_b, rec_a, rec_b, _acc, _top, *refs):
    outs, (acc, top, mix) = refs[:-3], refs[-3:]
    tasks, blocks, lives = [], [], []
    lives_own = []
    for pay, rec in zip((pay_a, pay_b), (rec_a, rec_b)):
        target, live_own, _home = read_flags(pay)
        block_in, live_in, _home = read_flags(rec)
        lives_own.append(live_own)
        q_far, gv_far = block_rows(rec, target)
        k_far, ov_far = block_rows(rec, 2)
        q_own, _gv = block_rows(pay, block_in)
        k_own, _ov = block_rows(pay, 2)
        tasks += [(k_far, q_own, ov_far), (q_far, k_own, gv_far)]
        blocks.append(block_in)
        lives.append(live_in)
    for i, parts in enumerate(attend(tasks)):
        if i % 2 == 0:
            fold(acc, top, blocks[i // 2], parts, lives[i // 2])
        else:
            fold(acc, top, 2 + i // 2, parts, True)
    if len(outs) == 1:
        mix = outs[0]
    slot_a, slot_b = slots()
    for index in range(4):
        if index < 2:
            chunk, first, live = 2 * index, 0, True
        else:
            slot = slot_a if index == 2 else slot_b
            chunk, first, live = 2 * slot, WIDTH, lives_own[index - 2]
        for h in range(HEADS):
            o = acc[index, h]
            l = o[HD : HD + 1]
            value = (o[:HD] * jnp.where(live & (l > 0), 1.0 / jnp.where(l > 0, l, 1.0), 0.0)).astype(jnp.bfloat16)
            at = first + h * HD
            mix[chunk, at : at + HD] = value[:, :128]
            mix[chunk + 1, at : at + HD] = value[:, 128:]
    if len(outs) > 1:
        for s, out in enumerate(outs):
            out[...] = mix[(lax.axis_index("head") + s) % GROUPS]


def apply_out(mixes, first, w):
    total = None
    for k in range(GROUPS):
        rows = mixes[k, pl.ds(pl.multiple_of(first, WIDTH), WIDTH)]
        piece = lax.dot_general(rows, w[k], TN, preferred_element_type=jnp.float32)
        piece = piece.astype(jnp.bfloat16).astype(jnp.float32)
        total = piece if total is None else total + piece
    return total.astype(jnp.bfloat16)


def own_out_kernel(mixes, w_own, out):
    out[...] = apply_out(mixes, parity() * WIDTH, w_own)


def other_out_kernel(mixes, w_other, own, grid_out, obs_out):
    other = apply_out(mixes, (1 - parity()) * WIDTH, w_other)
    first = parity() == 0
    grid_out[...] = jnp.where(first, own[...], other)
    obs_out[...] = jnp.where(first, other, own[...])


SMEM = pl.BlockSpec(memory_space=pltpu.SMEM)
VMEM = pl.BlockSpec(memory_space=pltpu.VMEM)
ANY = pl.BlockSpec(memory_space=pltpu.HBM)
PARAMS = pltpu.CompilerParams(vmem_limit_bytes=VMEM_LIMIT)


def in_hbm(x):
    return pltpu.with_memory_space_constraint(x, pltpu.HBM)


def in_vmem(x):
    return pltpu.with_memory_space_constraint(x, pltpu.VMEM)


def cost(flops, moved, exps=0):
    return pl.CostEstimate(flops=flops, bytes_accessed=moved, transcendentals=exps)


MIX_BY_PERMUTE = False


def body(
    grid_tokens, obs_tokens, w_query, w_gridval, w_key, w_obsval, w_gridout, w_obsout, obs_count, home_block, seam_block
):
    tiles = lax.axis_size("tile")
    swap_a = [(i, i ^ 1) for i in range(tiles)]
    swap_b = [(i, (i + 1) % tiles if i % 2 else (i - 1) % tiles) for i in range(tiles)]
    f32, bf16 = jnp.float32, jnp.bfloat16
    pay_shape = pltpu.VMEM((PAY, BS), bf16)
    pay_b_shape = pltpu.VMEM((PAY_B, BS), bf16)
    acc_shape = pltpu.VMEM((4, HEADS, ROWS_O, BS), f32)
    top_shape = pltpu.VMEM((4, HEADS, 8, BS), f32)
    mix_shape = jax.ShapeDtypeStruct((PAIR, 128), bf16)
    mixes_shape = pltpu.VMEM((GROUPS, PAIR, 128), bf16)
    w_shape = pltpu.VMEM((GROUPS, WIDTH, D), bf16)
    out_shape = jax.ShapeDtypeStruct((128, D), bf16)

    pay_a, pay_b, w_spread = pl.pallas_call(
        project_kernel,
        out_shape=(pay_shape, pay_b_shape, w_shape),
        in_specs=[pl.BlockSpec(memory_space=pl.ANY)] + [ANY] * 10,
        out_specs=(VMEM, VMEM, VMEM),
        scratch_shapes=[
            pltpu.VMEM((4 * BS, D), bf16),
            pltpu.VMEM((4 * WIDTH, D), bf16),
            pltpu.SMEM((2,), jnp.int32),
            pltpu.SMEM((2,), jnp.int32),
            pltpu.SMEM((1,), jnp.int32),
            pltpu.SemaphoreType.DMA((11,)),
        ],
        compiler_params=PARAMS,
        cost_estimate=cost(1, 1),
    )(
        obs_count,
        *map(
            in_hbm,
            (home_block, seam_block, grid_tokens, obs_tokens, w_query.T, w_gridval.T, w_key.T, w_obsval.T, w_gridout, w_obsout),
        ),
    )
    w_own = lax.all_to_all(w_spread, "head", split_axis=0, concat_axis=0, tiled=True)
    rec_b = lax.ppermute(pay_b, "tile", swap_b)
    acc, top = pl.pallas_call(
        home_kernel,
        out_shape=(acc_shape, top_shape),
        in_specs=[VMEM] * 2,
        out_specs=(VMEM, VMEM),
        compiler_params=PARAMS,
        cost_estimate=cost(3 * 10**9, 1),
    )(pay_a, pay_b)
    pay_a2 = pay_a
    rec_a = lax.ppermute(pay_a2, "tile", swap_a)
    count = GROUPS if MIX_BY_PERMUTE else 1
    mixes = pl.pallas_call(
        seam_kernel,
        out_shape=((mix_shape,) * GROUPS if MIX_BY_PERMUTE else (mixes_shape,)) + (acc_shape, top_shape),
        in_specs=[VMEM] * 6,
        out_specs=(VMEM,) * (count + 2),
        input_output_aliases={4: count, 5: count + 1},
        scratch_shapes=[pltpu.VMEM(mixes_shape.shape if MIX_BY_PERMUTE else (1, 16, 128), bf16)],
        compiler_params=PARAMS,
        cost_estimate=cost(1, 1),
    )(pay_a, pay_b, in_vmem(rec_a), in_vmem(rec_b), acc, top)
    late = mixes[0]
    late = mixes[0]
    if MIX_BY_PERMUTE:
        mixes = [mixes[0]] + [
            lax.ppermute(mixes[s], "head", [(i, (i + s) % GROUPS) for i in range(GROUPS)]) for s in (1, 2, 3)
        ]
    else:
        mixes = [lax.all_to_all(mixes[0], "head", split_axis=0, concat_axis=0, tiled=True)]
    w_own2, *_ = lax.optimization_barrier((w_own, late))
    w_other = lax.ppermute(w_own2, "tile", swap_a)
    own = pl.pallas_call(
        own_out_kernel,
        out_shape=pltpu.VMEM(out_shape.shape, bf16),
        in_specs=[VMEM] * 2,
        out_specs=VMEM,
        compiler_params=PARAMS,
        cost_estimate=cost(10**10, 1),
    )(in_vmem(mixes[0]), in_vmem(w_own))
    return pl.pallas_call(
        other_out_kernel,
        out_shape=(out_shape, out_shape),
        in_specs=[VMEM] * 3,
        out_specs=(VMEM, VMEM),
        compiler_params=PARAMS,
        cost_estimate=cost(1, 1),
    )(in_vmem(mixes[0]), in_vmem(w_other), own)


def solution(mesh):
    return jax.shard_map(
        body,
        mesh=mesh,
        in_specs=(
            P("tile", None),
            P("tile", None),
            P(None, "head"),
            P(None, "head"),
            P(None, "head"),
            P(None, "head"),
            P("head", None),
            P("head", None),
            P("tile"),
            P("tile"),
            P("tile"),
        ),
        out_specs=(P(("tile", "head"), None), P(("tile", "head"), None)),
        check_vma=False,
    )
```

```python
import jax
import jax.numpy as jnp
from jax import lax
from jax.experimental import pallas as pl
from jax.experimental.pallas import tpu as pltpu
from jax.sharding import PartitionSpec as P

HD = 64
BS = 256
HEADS = 3
WIDTH = HEADS * HD
PAIR = 2 * WIDTH
GROUPS = 4
D = 768
NEG = -1e30
ROWS_O = HD + 16
PAY = 3 * PAIR + 16
PAY_B = PAY + 16
NT = (((1,), (1,)), ((), ()))
TN = (((0,), (0,)), ((), ()))
VMEM_LIMIT = 48 * 1024 * 1024


def dot32(a, b):
    return jnp.dot(a, b, preferred_element_type=jnp.float32)


def parity():
    return lax.axis_index("tile") % 2


def slots():
    return 1 - parity(), parity()


def write_flags(pay, slot, count, home, seam):
    lane = lax.broadcasted_iota(jnp.int32, (16, BS), 1)
    live = (slot < count[0]).astype(jnp.int32)
    flags = jnp.where(lane < 64, seam[slot] & 1, jnp.where(lane < 128, live, home[slot]))
    pay[3 * PAIR : PAY] = flags.astype(jnp.float32).astype(jnp.bfloat16)


def read_flags(pay):
    flags = pay[3 * PAIR : PAY].astype(jnp.float32)
    target, live, home = (jnp.max(flags[:, 64 * i : 64 * (i + 1)]).astype(jnp.int32) for i in range(3))
    return target, live > 0, home


def project_kernel(
    count_any, home_hbm, seam_hbm, grid, obs, w_q, w_gv, w_k, w_ov, w_g, w_o, pay_a, pay_b, spread, tok, wts, wide, seam, home, count, sems
):
    slot_a, slot_b = slots()

    def rows(ref, block):
        return ref.at[pl.ds(pl.multiple_of(block * BS, BS), BS)]

    weights = (w_q, w_gv, w_k, w_ov)
    load_w = [pltpu.make_async_copy(w, wts.at[pl.ds(i * WIDTH, WIDTH)], sems.at[i]) for i, w in enumerate(weights)]
    load_g = pltpu.make_async_copy(grid, tok.at[pl.ds(0, 2 * BS)], sems.at[4])
    load_b = pltpu.make_async_copy(rows(obs, slot_b), tok.at[pl.ds(2 * BS, BS)], sems.at[5])
    load_a = pltpu.make_async_copy(rows(obs, slot_a), tok.at[pl.ds(3 * BS, BS)], sems.at[6])
    load_seam = pltpu.make_async_copy(seam_hbm, seam, sems.at[7])
    load_home = pltpu.make_async_copy(home_hbm, home, sems.at[10])
    load_count = pltpu.make_async_copy(count_any, count, sems.at[8])
    for copy in (load_w[0], load_w[1], load_g, load_w[2], load_w[3], load_b, load_a, load_seam, load_home, load_count):
        copy.start()

    load_s = [pltpu.make_async_copy(w, wide, sems.at[9]) for w in (w_g, w_o)]

    @pl.when(slot_b == 0)
    def _():
        load_s[0].start()

    @pl.when(slot_b == 1)
    def _():
        load_s[1].start()

    def project(i):
        w = wts[i * PAIR : (i + 1) * PAIR]
        t = tok[2 * i * BS : 2 * (i + 1) * BS]
        return lax.dot_general(w, t, NT, preferred_element_type=jnp.float32).astype(jnp.bfloat16)

    load_s[0].wait()
    send_s = [pltpu.make_async_copy(wide, spread.at[k], sems.at[11 + k]) for k in range(GROUPS)]
    for copy in send_s:
        copy.start()
    load_seam.wait()
    load_home.wait()
    load_count.wait()
    write_flags(pay_a, slot_a, count, home, seam)
    write_flags(pay_b, slot_b, count, home, seam)
    load_w[0].wait()
    load_w[1].wait()
    load_g.wait()
    x = project(0)
    for block in range(2):
        part = x[:, block * BS : (block + 1) * BS]
        pay_a[block * PAIR : (block + 1) * PAIR] = part
        pay_b[block * PAIR : (block + 1) * PAIR] = part
    load_w[2].wait()
    load_w[3].wait()
    load_b.wait()
    load_a.wait()
    x = project(1)
    pay_b[2 * PAIR : 3 * PAIR] = x[:, :BS]
    pay_a[2 * PAIR : 3 * PAIR] = x[:, BS:]
    for copy in send_s:
        copy.wait()


def attend(tasks):
    ones = jnp.ones((ROWS_O - HD, BS), jnp.bfloat16)
    heads = [slice(h * HD, (h + 1) * HD) for h in range(HEADS)]
    scores = []
    for rows_t, columns_t, _values in tasks:
        for at in heads:
            rows = jnp.transpose(rows_t[at]) * jnp.bfloat16(0.125)
            scores.append(dot32(rows, columns_t[at]))
    parts = []
    for index, s in enumerate(scores):
        values = tasks[index // HEADS][2][heads[index % HEADS]]
        m = jnp.max(s, axis=0, keepdims=True)
        e = jnp.exp(s - m).astype(jnp.bfloat16)
        parts.append((dot32(jnp.concatenate([values, ones], axis=0), e), m))
    return [parts[HEADS * t : HEADS * (t + 1)] for t in range(len(tasks))]


def fold(acc, top, index, parts, live):
    for h, (o, m) in enumerate(parts):
        old = top[index, h, :1]
        new = jnp.where(live, jnp.maximum(old, m), old)
        weight = jnp.where(live, jnp.exp(m - new), 0.0)
        acc[index, h] = acc[index, h] * jnp.exp(old - new) + o * weight
        top[index, h] = jnp.broadcast_to(new, (8, BS))


def block_rows(ref, block):
    start = pl.multiple_of(block * PAIR, WIDTH)
    return ref[pl.ds(start, WIDTH)], ref[pl.ds(pl.multiple_of(start + WIDTH, WIDTH), WIDTH)]


def home_kernel(pay_a, pay_b, acc, top):
    tasks, blocks, lives = [], [], []
    for pay in (pay_a, pay_b):
        _target, live, block = read_flags(pay)
        q_t, gv_t = block_rows(pay, block)
        k_t, ov_t = block_rows(pay, 2)
        tasks += [(k_t, q_t, ov_t), (q_t, k_t, gv_t)]
        blocks.append(block)
        lives.append(live)
    grid_a, obs_a, grid_b, obs_b = attend(tasks)
    for index, parts in ((2, obs_a), (3, obs_b)):
        for h, (o, m) in enumerate(parts):
            acc[index, h] = o
            top[index, h] = jnp.broadcast_to(m, (8, BS))
    for block in range(2):
        used = [(b == block) & live for b, live in zip(blocks, lives)]
        for h in range(HEADS):
            pair = (grid_a[h], grid_b[h])
            new = jnp.maximum(*[jnp.where(u, m, NEG) for u, (_o, m) in zip(used, pair)])
            first, second = [o * jnp.where(u, jnp.exp(m - new), 0.0) for u, (o, m) in zip(used, pair)]
            acc[block, h] = first + second
            top[block, h] = jnp.broadcast_to(new, (8, BS))


def seam_kernel(pay_a, pay_b, rec_a, rec_b, _acc, _top, *refs):
    outs, (acc, top, mix) = refs[:-3], refs[-3:]
    tasks, blocks, lives = [], [], []
    lives_own = []
    for pay, rec in zip((pay_a, pay_b), (rec_a, rec_b)):
        target, live_own, _home = read_flags(pay)
        block_in, live_in, _home = read_flags(rec)
        lives_own.append(live_own)
        q_far, gv_far = block_rows(rec, target)
        k_far, ov_far = block_rows(rec, 2)
        q_own, _gv = block_rows(pay, block_in)
        k_own, _ov = block_rows(pay, 2)
        tasks += [(k_far, q_own, ov_far), (q_far, k_own, gv_far)]
        blocks.append(block_in)
        lives.append(live_in)
    for i, parts in enumerate(attend(tasks)):
        if i % 2 == 0:
            fold(acc, top, blocks[i // 2], parts, lives[i // 2])
        else:
            fold(acc, top, 2 + i // 2, parts, True)
    if len(outs) == 1:
        mix = outs[0]
    slot_a, slot_b = slots()
    for index in range(4):
        if index < 2:
            chunk, first, live = 2 * index, 0, True
        else:
            slot = slot_a if index == 2 else slot_b
            chunk, first, live = 2 * slot, WIDTH, lives_own[index - 2]
        for h in range(HEADS):
            o = acc[index, h]
            l = o[HD : HD + 1]
            value = (o[:HD] * jnp.where(live & (l > 0), 1.0 / jnp.where(l > 0, l, 1.0), 0.0)).astype(jnp.bfloat16)
            at = first + h * HD
            mix[chunk, at : at + HD] = value[:, :128]
            mix[chunk + 1, at : at + HD] = value[:, 128:]
    if len(outs) > 1:
        for s, out in enumerate(outs):
            out[...] = mix[(lax.axis_index("head") + s) % GROUPS]


def apply_out(mixes, first, w):
    total = None
    for k in range(GROUPS):
        rows = mixes[k, pl.ds(pl.multiple_of(first, WIDTH), WIDTH)]
        piece = lax.dot_general(rows, w[k], TN, preferred_element_type=jnp.float32)
        piece = piece.astype(jnp.bfloat16).astype(jnp.float32)
        total = piece if total is None else total + piece
    return total.astype(jnp.bfloat16)


def own_out_kernel(mixes, w_own, out):
    out[...] = apply_out(mixes, parity() * WIDTH, w_own)


def other_out_kernel(mixes, w_other, own, grid_out, obs_out):
    other = apply_out(mixes, (1 - parity()) * WIDTH, w_other)
    first = parity() == 0
    grid_out[...] = jnp.where(first, own[...], other)
    obs_out[...] = jnp.where(first, other, own[...])


SMEM = pl.BlockSpec(memory_space=pltpu.SMEM)
VMEM = pl.BlockSpec(memory_space=pltpu.VMEM)
ANY = pl.BlockSpec(memory_space=pltpu.HBM)
PARAMS = pltpu.CompilerParams(vmem_limit_bytes=VMEM_LIMIT)


def in_hbm(x):
    return pltpu.with_memory_space_constraint(x, pltpu.HBM)


def in_vmem(x):
    return pltpu.with_memory_space_constraint(x, pltpu.VMEM)


def cost(flops, moved, exps=0):
    return pl.CostEstimate(flops=flops, bytes_accessed=moved, transcendentals=exps)


MIX_BY_PERMUTE = False


def body(
    grid_tokens, obs_tokens, w_query, w_gridval, w_key, w_obsval, w_gridout, w_obsout, obs_count, home_block, seam_block
):
    tiles = lax.axis_size("tile")
    swap_a = [(i, i ^ 1) for i in range(tiles)]
    swap_b = [(i, (i + 1) % tiles if i % 2 else (i - 1) % tiles) for i in range(tiles)]
    f32, bf16 = jnp.float32, jnp.bfloat16
    pay_shape = pltpu.VMEM((PAY, BS), bf16)
    pay_b_shape = pltpu.VMEM((PAY_B, BS), bf16)
    acc_shape = pltpu.VMEM((4, HEADS, ROWS_O, BS), f32)
    top_shape = pltpu.VMEM((4, HEADS, 8, BS), f32)
    mix_shape = jax.ShapeDtypeStruct((PAIR, 128), bf16)
    mixes_shape = pltpu.VMEM((GROUPS, PAIR, 128), bf16)
    w_shape = pltpu.HBM((GROUPS, WIDTH, D), bf16)
    out_shape = jax.ShapeDtypeStruct((128, D), bf16)

    pay_a, pay_b, w_spread = pl.pallas_call(
        project_kernel,
        out_shape=(pay_shape, pay_b_shape, w_shape),
        in_specs=[pl.BlockSpec(memory_space=pl.ANY)] + [ANY] * 10,
        out_specs=(VMEM, VMEM, ANY),
        scratch_shapes=[
            pltpu.VMEM((4 * BS, D), bf16),
            pltpu.VMEM((4 * WIDTH, D), bf16),
            pltpu.VMEM((WIDTH, D), bf16),
            pltpu.SMEM((2,), jnp.int32),
            pltpu.SMEM((2,), jnp.int32),
            pltpu.SMEM((1,), jnp.int32),
            pltpu.SemaphoreType.DMA((11 + GROUPS,)),
        ],
        compiler_params=PARAMS,
        cost_estimate=cost(1, 1),
    )(
        obs_count,
        *map(
            in_hbm,
            (home_block, seam_block, grid_tokens, obs_tokens, w_query.T, w_gridval.T, w_key.T, w_obsval.T, w_gridout, w_obsout),
        ),
    )
    w_own = lax.all_to_all(w_spread, "head", split_axis=0, concat_axis=0, tiled=True)
    rec_b = lax.ppermute(pay_b, "tile", swap_b)
    acc, top = pl.pallas_call(
        home_kernel,
        out_shape=(acc_shape, top_shape),
        in_specs=[VMEM] * 2,
        out_specs=(VMEM, VMEM),
        compiler_params=PARAMS,
        cost_estimate=cost(3 * 10**9, 1),
    )(pay_a, pay_b)
    pay_a2 = pay_a
    rec_a = lax.ppermute(pay_a2, "tile", swap_a)
    count = GROUPS if MIX_BY_PERMUTE else 1
    mixes = pl.pallas_call(
        seam_kernel,
        out_shape=((mix_shape,) * GROUPS if MIX_BY_PERMUTE else (mixes_shape,)) + (acc_shape, top_shape),
        in_specs=[VMEM] * 6,
        out_specs=(VMEM,) * (count + 2),
        input_output_aliases={4: count, 5: count + 1},
        scratch_shapes=[pltpu.VMEM(mixes_shape.shape if MIX_BY_PERMUTE else (1, 16, 128), bf16)],
        compiler_params=PARAMS,
        cost_estimate=cost(1, 1),
    )(pay_a, pay_b, in_vmem(rec_a), in_vmem(rec_b), acc, top)
    late = mixes[0]
    late = mixes[0]
    if MIX_BY_PERMUTE:
        mixes = [mixes[0]] + [
            lax.ppermute(mixes[s], "head", [(i, (i + s) % GROUPS) for i in range(GROUPS)]) for s in (1, 2, 3)
        ]
    else:
        mixes = [lax.all_to_all(mixes[0], "head", split_axis=0, concat_axis=0, tiled=True)]
    w_own2, *_ = lax.optimization_barrier((w_own, late))
    w_other = lax.ppermute(w_own2, "tile", swap_a)
    own = pl.pallas_call(
        own_out_kernel,
        out_shape=pltpu.VMEM(out_shape.shape, bf16),
        in_specs=[VMEM] * 2,
        out_specs=VMEM,
        compiler_params=PARAMS,
        cost_estimate=cost(10**10, 1),
    )(in_vmem(mixes[0]), in_vmem(w_own))
    return pl.pallas_call(
        other_out_kernel,
        out_shape=(out_shape, out_shape),
        in_specs=[VMEM] * 3,
        out_specs=(VMEM, VMEM),
        compiler_params=PARAMS,
        cost_estimate=cost(1, 1),
    )(in_vmem(mixes[0]), in_vmem(w_other), own)


def solution(mesh):
    return jax.shard_map(
        body,
        mesh=mesh,
        in_specs=(
            P("tile", None),
            P("tile", None),
            P(None, "head"),
            P(None, "head"),
            P(None, "head"),
            P(None, "head"),
            P("head", None),
            P("head", None),
            P("tile"),
            P("tile"),
            P("tile"),
        ),
        out_specs=(P(("tile", "head"), None), P(("tile", "head"), None)),
        check_vma=False,
    )
```

```python
import jax
import jax.numpy as jnp
from jax import lax
from jax.experimental import pallas as pl
from jax.experimental.pallas import tpu as pltpu
from jax.sharding import PartitionSpec as P

HD = 64
BS = 256
HEADS = 3
WIDTH = HEADS * HD
PAIR = 2 * WIDTH
GROUPS = 4
D = 768
NEG = -1e30
ROWS_O = HD + 16
PAY = 3 * PAIR + 16
PAY_B = PAY + 16
NT = (((1,), (1,)), ((), ()))
TN = (((0,), (0,)), ((), ()))
VMEM_LIMIT = 48 * 1024 * 1024


def dot32(a, b):
    return jnp.dot(a, b, preferred_element_type=jnp.float32)


def parity():
    return lax.axis_index("tile") % 2


def slots():
    return 1 - parity(), parity()


def write_flags(pay, slot, count, home, seam):
    lane = lax.broadcasted_iota(jnp.int32, (16, BS), 1)
    live = (slot < count[0]).astype(jnp.int32)
    flags = jnp.where(lane < 64, seam[slot] & 1, jnp.where(lane < 128, live, home[slot]))
    pay[3 * PAIR : PAY] = flags.astype(jnp.float32).astype(jnp.bfloat16)


def read_flags(pay):
    flags = pay[3 * PAIR : PAY].astype(jnp.float32)
    target, live, home = (jnp.max(flags[:, 64 * i : 64 * (i + 1)]).astype(jnp.int32) for i in range(3))
    return target, live > 0, home


def project_kernel(
    count_any, home_hbm, seam_hbm, grid, obs, w_q, w_gv, w_k, w_ov, w_g, w_o, pay_a, pay_b, spread, tok, wts, wide, seam, home, count, sems
):
    slot_a, slot_b = slots()

    def rows(ref, block):
        return ref.at[pl.ds(pl.multiple_of(block * BS, BS), BS)]

    weights = (w_q, w_gv, w_k, w_ov)
    load_w = [pltpu.make_async_copy(w, wts.at[pl.ds(i * WIDTH, WIDTH)], sems.at[i]) for i, w in enumerate(weights)]
    load_g = pltpu.make_async_copy(grid, tok.at[pl.ds(0, 2 * BS)], sems.at[4])
    load_b = pltpu.make_async_copy(rows(obs, slot_b), tok.at[pl.ds(2 * BS, BS)], sems.at[5])
    load_a = pltpu.make_async_copy(rows(obs, slot_a), tok.at[pl.ds(3 * BS, BS)], sems.at[6])
    load_seam = pltpu.make_async_copy(seam_hbm, seam, sems.at[7])
    load_home = pltpu.make_async_copy(home_hbm, home, sems.at[10])
    load_count = pltpu.make_async_copy(count_any, count, sems.at[8])
    for copy in (load_w[0], load_w[1], load_g, load_w[2], load_w[3], load_b, load_a, load_seam, load_home, load_count):
        copy.start()

    load_s = [pltpu.make_async_copy(w, wide, sems.at[9]) for w in (w_g, w_o)]

    @pl.when(slot_b == 0)
    def _():
        load_s[0].start()

    @pl.when(slot_b == 1)
    def _():
        load_s[1].start()

    def project(i):
        w = wts[i * PAIR : (i + 1) * PAIR]
        t = tok[2 * i * BS : 2 * (i + 1) * BS]
        return lax.dot_general(w, t, NT, preferred_element_type=jnp.float32).astype(jnp.bfloat16)

    load_s[0].wait()
    send_s = [pltpu.make_async_copy(wide, spread.at[k], sems.at[11 + k]) for k in range(GROUPS)]
    for copy in send_s:
        copy.start()
    load_seam.wait()
    load_home.wait()
    load_count.wait()
    write_flags(pay_a, slot_a, count, home, seam)
    write_flags(pay_b, slot_b, count, home, seam)
    load_w[0].wait()
    load_w[1].wait()
    load_g.wait()
    x = project(0)
    for block in range(2):
        part = x[:, block * BS : (block + 1) * BS]
        pay_a[block * PAIR : (block + 1) * PAIR] = part
        pay_b[block * PAIR : (block + 1) * PAIR] = part
    load_w[2].wait()
    load_w[3].wait()
    load_b.wait()
    load_a.wait()
    x = project(1)
    pay_b[2 * PAIR : 3 * PAIR] = x[:, :BS]
    pay_a[2 * PAIR : 3 * PAIR] = x[:, BS:]
    for copy in send_s:
        copy.wait()


def attend(tasks):
    ones = jnp.ones((ROWS_O - HD, BS), jnp.bfloat16)
    heads = [slice(h * HD, (h + 1) * HD) for h in range(HEADS)]
    scores = []
    for rows_t, columns_t, _values in tasks:
        for at in heads:
            rows = jnp.transpose(rows_t[at]) * jnp.bfloat16(0.125)
            scores.append(dot32(rows, columns_t[at]))
    parts = []
    for index, s in enumerate(scores):
        values = tasks[index // HEADS][2][heads[index % HEADS]]
        m = jnp.max(s, axis=0, keepdims=True)
        e = jnp.exp(s - m).astype(jnp.bfloat16)
        parts.append((dot32(jnp.concatenate([values, ones], axis=0), e), m))
    return [parts[HEADS * t : HEADS * (t + 1)] for t in range(len(tasks))]


def fold(acc, top, index, parts, live):
    for h, (o, m) in enumerate(parts):
        old = top[index, h, :1]
        new = jnp.where(live, jnp.maximum(old, m), old)
        more = jnp.where(live, o * jnp.exp(m - new), 0.0)
        acc[index, h] = acc[index, h] * jnp.exp(old - new) + more
        top[index, h] = jnp.broadcast_to(new, (8, BS))


def block_rows(ref, block):
    start = pl.multiple_of(block * PAIR, WIDTH)
    return ref[pl.ds(start, WIDTH)], ref[pl.ds(pl.multiple_of(start + WIDTH, WIDTH), WIDTH)]


def home_kernel(pay_a, pay_b, acc, top):
    tasks, blocks, lives = [], [], []
    for pay in (pay_a, pay_b):
        _target, live, block = read_flags(pay)
        q_t, gv_t = block_rows(pay, block)
        k_t, ov_t = block_rows(pay, 2)
        tasks += [(k_t, q_t, ov_t), (q_t, k_t, gv_t)]
        blocks.append(block)
        lives.append(live)
    grid_a, obs_a, grid_b, obs_b = attend(tasks)
    for index, parts in ((2, obs_a), (3, obs_b)):
        for h, (o, m) in enumerate(parts):
            acc[index, h] = o
            top[index, h] = jnp.broadcast_to(m, (8, BS))
    for block in range(2):
        used = [(b == block) & live for b, live in zip(blocks, lives)]
        for h in range(HEADS):
            pair = (grid_a[h], grid_b[h])
            new = jnp.maximum(*[jnp.where(u, m, NEG) for u, (_o, m) in zip(used, pair)])
            first, second = [jnp.where(u, o * jnp.exp(m - new), 0.0) for u, (o, m) in zip(used, pair)]
            acc[block, h] = first + second
            top[block, h] = jnp.broadcast_to(new, (8, BS))


def seam_kernel(pay_a, pay_b, rec_a, rec_b, _acc, _top, *refs):
    outs, (acc, top, mix) = refs[:-3], refs[-3:]
    tasks, blocks, lives = [], [], []
    lives_own = []
    for pay, rec in zip((pay_a, pay_b), (rec_a, rec_b)):
        target, live_own, _home = read_flags(pay)
        block_in, live_in, _home = read_flags(rec)
        lives_own.append(live_own)
        q_far, gv_far = block_rows(rec, target)
        k_far, ov_far = block_rows(rec, 2)
        q_own, _gv = block_rows(pay, block_in)
        k_own, _ov = block_rows(pay, 2)
        tasks += [(k_far, q_own, ov_far), (q_far, k_own, gv_far)]
        blocks.append(block_in)
        lives.append(live_in)
    for i, parts in enumerate(attend(tasks)):
        if i % 2 == 0:
            fold(acc, top, blocks[i // 2], parts, lives[i // 2])
        else:
            fold(acc, top, 2 + i // 2, parts, True)
    if len(outs) == 1:
        mix = outs[0]
    slot_a, slot_b = slots()
    for index in range(4):
        if index < 2:
            chunk, first, live = 2 * index, 0, True
        else:
            slot = slot_a if index == 2 else slot_b
            chunk, first, live = 2 * slot, WIDTH, lives_own[index - 2]
        for h in range(HEADS):
            o = acc[index, h]
            l = o[HD : HD + 1]
            value = jnp.where(live & (l > 0), o[:HD] / jnp.where(l > 0, l, 1.0), 0.0).astype(jnp.bfloat16)
            at = first + h * HD
            mix[chunk, at : at + HD] = value[:, :128]
            mix[chunk + 1, at : at + HD] = value[:, 128:]
    if len(outs) > 1:
        for s, out in enumerate(outs):
            out[...] = mix[(lax.axis_index("head") + s) % GROUPS]


def apply_out(mixes, first, w):
    total = None
    for k in range(GROUPS):
        rows = mixes[k, pl.ds(pl.multiple_of(first, WIDTH), WIDTH)]
        piece = lax.dot_general(rows, w[k], TN, preferred_element_type=jnp.float32)
        piece = piece.astype(jnp.bfloat16).astype(jnp.float32)
        total = piece if total is None else total + piece
    return total.astype(jnp.bfloat16)


def own_out_kernel(mixes, w_own, out):
    out[...] = apply_out(mixes, parity() * WIDTH, w_own)


def other_out_kernel(mixes, w_other, own, grid_out, obs_out):
    other = apply_out(mixes, (1 - parity()) * WIDTH, w_other)
    first = parity() == 0
    grid_out[...] = jnp.where(first, own[...], other)
    obs_out[...] = jnp.where(first, other, own[...])


SMEM = pl.BlockSpec(memory_space=pltpu.SMEM)
VMEM = pl.BlockSpec(memory_space=pltpu.VMEM)
ANY = pl.BlockSpec(memory_space=pltpu.HBM)
PARAMS = pltpu.CompilerParams(vmem_limit_bytes=VMEM_LIMIT)


def in_hbm(x):
    return pltpu.with_memory_space_constraint(x, pltpu.HBM)


def in_vmem(x):
    return pltpu.with_memory_space_constraint(x, pltpu.VMEM)


def cost(flops, moved, exps=0):
    return pl.CostEstimate(flops=flops, bytes_accessed=moved, transcendentals=exps)


MIX_BY_PERMUTE = False


def body(
    grid_tokens, obs_tokens, w_query, w_gridval, w_key, w_obsval, w_gridout, w_obsout, obs_count, home_block, seam_block
):
    tiles = lax.axis_size("tile")
    swap_a = [(i, i ^ 1) for i in range(tiles)]
    swap_b = [(i, (i + 1) % tiles if i % 2 else (i - 1) % tiles) for i in range(tiles)]
    f32, bf16 = jnp.float32, jnp.bfloat16
    pay_shape = pltpu.VMEM((PAY, BS), bf16)
    pay_b_shape = pltpu.VMEM((PAY_B, BS), bf16)
    acc_shape = pltpu.VMEM((4, HEADS, ROWS_O, BS), f32)
    top_shape = pltpu.VMEM((4, HEADS, 8, BS), f32)
    mix_shape = jax.ShapeDtypeStruct((PAIR, 128), bf16)
    mixes_shape = pltpu.VMEM((GROUPS, PAIR, 128), bf16)
    w_shape = pltpu.HBM((GROUPS, WIDTH, D), bf16)
    out_shape = jax.ShapeDtypeStruct((128, D), bf16)

    pay_a, pay_b, w_spread = pl.pallas_call(
        project_kernel,
        out_shape=(pay_shape, pay_b_shape, w_shape),
        in_specs=[pl.BlockSpec(memory_space=pl.ANY)] + [ANY] * 10,
        out_specs=(VMEM, VMEM, ANY),
        scratch_shapes=[
            pltpu.VMEM((4 * BS, D), bf16),
            pltpu.VMEM((4 * WIDTH, D), bf16),
            pltpu.VMEM((WIDTH, D), bf16),
            pltpu.SMEM((2,), jnp.int32),
            pltpu.SMEM((2,), jnp.int32),
            pltpu.SMEM((1,), jnp.int32),
            pltpu.SemaphoreType.DMA((11 + GROUPS,)),
        ],
        compiler_params=PARAMS,
        cost_estimate=cost(1, 1),
    )(
        obs_count,
        *map(
            in_hbm,
            (home_block, seam_block, grid_tokens, obs_tokens, w_query.T, w_gridval.T, w_key.T, w_obsval.T, w_gridout, w_obsout),
        ),
    )
    w_own = lax.all_to_all(w_spread, "head", split_axis=0, concat_axis=0, tiled=True)
    rec_b = lax.ppermute(pay_b, "tile", swap_b)
    acc, top = pl.pallas_call(
        home_kernel,
        out_shape=(acc_shape, top_shape),
        in_specs=[VMEM] * 2,
        out_specs=(VMEM, VMEM),
        compiler_params=PARAMS,
        cost_estimate=cost(3 * 10**9, 1),
    )(pay_a, pay_b)
    pay_a2 = pay_a
    rec_a = lax.ppermute(pay_a2, "tile", swap_a)
    count = GROUPS if MIX_BY_PERMUTE else 1
    mixes = pl.pallas_call(
        seam_kernel,
        out_shape=((mix_shape,) * GROUPS if MIX_BY_PERMUTE else (mixes_shape,)) + (acc_shape, top_shape),
        in_specs=[VMEM] * 6,
        out_specs=(VMEM,) * (count + 2),
        input_output_aliases={4: count, 5: count + 1},
        scratch_shapes=[pltpu.VMEM(mixes_shape.shape if MIX_BY_PERMUTE else (1, 16, 128), bf16)],
        compiler_params=PARAMS,
        cost_estimate=cost(1, 1),
    )(pay_a, pay_b, in_vmem(rec_a), in_vmem(rec_b), acc, top)
    late = mixes[0]
    late = mixes[0]
    if MIX_BY_PERMUTE:
        mixes = [mixes[0]] + [
            lax.ppermute(mixes[s], "head", [(i, (i + s) % GROUPS) for i in range(GROUPS)]) for s in (1, 2, 3)
        ]
    else:
        mixes = [lax.all_to_all(mixes[0], "head", split_axis=0, concat_axis=0, tiled=True)]
    w_own2, *_ = lax.optimization_barrier((w_own, late))
    w_other = lax.ppermute(w_own2, "tile", swap_a)
    own = pl.pallas_call(
        own_out_kernel,
        out_shape=pltpu.VMEM(out_shape.shape, bf16),
        in_specs=[VMEM] * 2,
        out_specs=VMEM,
        compiler_params=PARAMS,
        cost_estimate=cost(10**10, 1),
    )(in_vmem(mixes[0]), in_vmem(w_own))
    return pl.pallas_call(
        other_out_kernel,
        out_shape=(out_shape, out_shape),
        in_specs=[VMEM] * 3,
        out_specs=(VMEM, VMEM),
        compiler_params=PARAMS,
        cost_estimate=cost(1, 1),
    )(in_vmem(mixes[0]), in_vmem(w_other), own)


def solution(mesh):
    return jax.shard_map(
        body,
        mesh=mesh,
        in_specs=(
            P("tile", None),
            P("tile", None),
            P(None, "head"),
            P(None, "head"),
            P(None, "head"),
            P(None, "head"),
            P("head", None),
            P("head", None),
            P("tile"),
            P("tile"),
            P("tile"),
        ),
        out_specs=(P(("tile", "head"), None), P(("tile", "head"), None)),
        check_vma=False,
    )
```

```python
import jax
import jax.numpy as jnp
from jax import lax
from jax.experimental import pallas as pl
from jax.experimental.pallas import tpu as pltpu
from jax.sharding import PartitionSpec as P

HD = 64
BS = 256
HEADS = 3
WIDTH = HEADS * HD
PAIR = 2 * WIDTH
GROUPS = 4
D = 768
NEG = -1e30
ROWS_O = HD + 16
PAY = 3 * PAIR + 16
PAY_B = PAY + 16
NT = (((1,), (1,)), ((), ()))
TN = (((0,), (0,)), ((), ()))
VMEM_LIMIT = 48 * 1024 * 1024


def dot32(a, b):
    return jnp.dot(a, b, preferred_element_type=jnp.float32)


def parity():
    return lax.axis_index("tile") % 2


def slots():
    return 1 - parity(), parity()


def write_flags(pay, slot, count, home, seam):
    lane = lax.broadcasted_iota(jnp.int32, (16, BS), 1)
    live = (slot < count[0]).astype(jnp.int32)
    flags = jnp.where(lane < 64, seam[slot] & 1, jnp.where(lane < 128, live, home[slot]))
    pay[3 * PAIR : PAY] = flags.astype(jnp.float32).astype(jnp.bfloat16)


def read_flags(pay):
    flags = pay[3 * PAIR : PAY].astype(jnp.float32)
    target, live, home = (jnp.max(flags[:, 64 * i : 64 * (i + 1)]).astype(jnp.int32) for i in range(3))
    return target, live > 0, home


def project_kernel(
    count_any, home_hbm, seam_hbm, grid, obs, w_q, w_gv, w_k, w_ov, w_g, w_o, pay_a, pay_b, spread, tok, wts, wide, seam, home, count, sems
):
    slot_a, slot_b = slots()

    def rows(ref, block):
        return ref.at[pl.ds(pl.multiple_of(block * BS, BS), BS)]

    weights = (w_q, w_gv, w_k, w_ov)
    load_w = [pltpu.make_async_copy(w, wts.at[pl.ds(i * WIDTH, WIDTH)], sems.at[i]) for i, w in enumerate(weights)]
    load_g = pltpu.make_async_copy(grid, tok.at[pl.ds(0, 2 * BS)], sems.at[4])
    load_b = pltpu.make_async_copy(rows(obs, slot_b), tok.at[pl.ds(2 * BS, BS)], sems.at[5])
    load_a = pltpu.make_async_copy(rows(obs, slot_a), tok.at[pl.ds(3 * BS, BS)], sems.at[6])
    load_seam = pltpu.make_async_copy(seam_hbm, seam, sems.at[7])
    load_home = pltpu.make_async_copy(home_hbm, home, sems.at[10])
    load_count = pltpu.make_async_copy(count_any, count, sems.at[8])
    for copy in (load_w[0], load_w[1], load_g, load_w[2], load_w[3], load_b, load_a, load_seam, load_home, load_count):
        copy.start()

    load_s = [pltpu.make_async_copy(w, wide, sems.at[9]) for w in (w_g, w_o)]

    @pl.when(slot_b == 0)
    def _():
        load_s[0].start()

    @pl.when(slot_b == 1)
    def _():
        load_s[1].start()

    def project(i):
        w = wts[i * PAIR : (i + 1) * PAIR]
        t = tok[2 * i * BS : 2 * (i + 1) * BS]
        return lax.dot_general(w, t, NT, preferred_element_type=jnp.float32).astype(jnp.bfloat16)

    load_s[0].wait()
    send_s = [pltpu.make_async_copy(wide, spread.at[k], sems.at[11 + k]) for k in range(GROUPS)]
    for copy in send_s:
        copy.start()
    load_seam.wait()
    load_home.wait()
    load_count.wait()
    write_flags(pay_a, slot_a, count, home, seam)
    write_flags(pay_b, slot_b, count, home, seam)
    load_w[0].wait()
    load_w[1].wait()
    load_g.wait()
    x = project(0)
    for block in range(2):
        part = x[:, block * BS : (block + 1) * BS]
        pay_a[block * PAIR : (block + 1) * PAIR] = part
        pay_b[block * PAIR : (block + 1) * PAIR] = part
    load_w[2].wait()
    load_w[3].wait()
    load_b.wait()
    load_a.wait()
    x = project(1)
    pay_b[2 * PAIR : 3 * PAIR] = x[:, :BS]
    pay_a[2 * PAIR : 3 * PAIR] = x[:, BS:]
    for copy in send_s:
        copy.wait()


def attend(tasks):
    ones = jnp.ones((ROWS_O - HD, BS), jnp.bfloat16)
    heads = [slice(h * HD, (h + 1) * HD) for h in range(HEADS)]
    scores = []
    for rows_t, columns_t, _values in tasks:
        for at in heads:
            rows = jnp.transpose(rows_t[at]) * jnp.bfloat16(0.125)
            scores.append(dot32(rows, columns_t[at]))
    parts = []
    for index, s in enumerate(scores):
        values = tasks[index // HEADS][2][heads[index % HEADS]]
        m = jnp.max(s, axis=0, keepdims=True)
        e = jnp.exp(s - m).astype(jnp.bfloat16)
        parts.append((dot32(jnp.concatenate([values, ones], axis=0), e), m))
    return [parts[HEADS * t : HEADS * (t + 1)] for t in range(len(tasks))]


def fold(acc, top, index, parts, live):
    for h, (o, m) in enumerate(parts):
        old = top[index, h, :1]
        new = jnp.where(live, jnp.maximum(old, m), old)
        more = jnp.where(live, o * jnp.exp(m - new), 0.0)
        acc[index, h] = acc[index, h] * jnp.exp(old - new) + more
        top[index, h] = jnp.broadcast_to(new, (8, BS))


def block_rows(ref, block):
    start = pl.multiple_of(block * PAIR, WIDTH)
    return ref[pl.ds(start, WIDTH)], ref[pl.ds(pl.multiple_of(start + WIDTH, WIDTH), WIDTH)]


def home_kernel(pay_a, pay_b, acc, top):
    tasks, blocks, lives = [], [], []
    for pay in (pay_a, pay_b):
        _target, live, block = read_flags(pay)
        q_t, gv_t = block_rows(pay, block)
        k_t, ov_t = block_rows(pay, 2)
        tasks += [(k_t, q_t, ov_t), (q_t, k_t, gv_t)]
        blocks.append(block)
        lives.append(live)
    grid_a, obs_a, grid_b, obs_b = attend(tasks)
    for index, parts in ((2, obs_a), (3, obs_b)):
        for h, (o, m) in enumerate(parts):
            acc[index, h] = o
            top[index, h] = jnp.broadcast_to(m, (8, BS))
    for block in range(2):
        used = [(b == block) & live for b, live in zip(blocks, lives)]
        for h in range(HEADS):
            pair = (grid_a[h], grid_b[h])
            new = jnp.maximum(*[jnp.where(u, m, NEG) for u, (_o, m) in zip(used, pair)])
            first, second = [jnp.where(u, o * jnp.exp(m - new), 0.0) for u, (o, m) in zip(used, pair)]
            acc[block, h] = first + second
            top[block, h] = jnp.broadcast_to(new, (8, BS))


def seam_kernel(pay_a, pay_b, rec_a, rec_b, _acc, _top, *refs):
    out, acc, top, mix, sems = refs
    tasks, blocks, lives = [], [], []
    lives_own = []
    for pay, rec in zip((pay_a, pay_b), (rec_a, rec_b)):
        target, live_own, _home = read_flags(pay)
        block_in, live_in, _home = read_flags(rec)
        lives_own.append(live_own)
        q_far, gv_far = block_rows(rec, target)
        k_far, ov_far = block_rows(rec, 2)
        q_own, _gv = block_rows(pay, block_in)
        k_own, _ov = block_rows(pay, 2)
        tasks += [(k_far, q_own, ov_far), (q_far, k_own, gv_far)]
        blocks.append(block_in)
        lives.append(live_in)
    for i, parts in enumerate(attend(tasks)):
        if i % 2 == 0:
            fold(acc, top, blocks[i // 2], parts, lives[i // 2])
        else:
            fold(acc, top, 2 + i // 2, parts, True)
    slot_a, slot_b = slots()
    stores = []
    for index in (2, 3, 0, 1):
        if index < 2:
            chunk, first, live = 2 * index, 0, True
        else:
            slot = slot_a if index == 2 else slot_b
            chunk, first, live = 2 * slot, WIDTH, lives_own[index - 2]
        for h in range(HEADS):
            o = acc[index, h]
            l = o[HD : HD + 1]
            value = jnp.where(live & (l > 0), o[:HD] / jnp.where(l > 0, l, 1.0), 0.0).astype(jnp.bfloat16)
            at = first + h * HD
            mix[chunk, at : at + HD] = value[:, :128]
            mix[chunk + 1, at : at + HD] = value[:, 128:]
        if index in (3, 1):
            part = (slice(None), pl.ds(first, WIDTH))
            stores.append(pltpu.make_async_copy(mix.at[part], out.at[part], sems.at[len(stores)]))
            stores[-1].start()
    for copy in stores:
        copy.wait()


def apply_out(mixes, first, w):
    total = None
    for k in range(GROUPS):
        rows = mixes[k, pl.ds(pl.multiple_of(first, WIDTH), WIDTH)]
        piece = lax.dot_general(rows, w[k], TN, preferred_element_type=jnp.float32)
        piece = piece.astype(jnp.bfloat16).astype(jnp.float32)
        total = piece if total is None else total + piece
    return total.astype(jnp.bfloat16)


def own_out_kernel(mixes, w_own, out):
    out[...] = apply_out(mixes, parity() * WIDTH, w_own)


def other_out_kernel(mixes, w_other, own, grid_out, obs_out):
    other = apply_out(mixes, (1 - parity()) * WIDTH, w_other)
    first = parity() == 0
    grid_out[...] = jnp.where(first, own[...], other)
    obs_out[...] = jnp.where(first, other, own[...])


SMEM = pl.BlockSpec(memory_space=pltpu.SMEM)
VMEM = pl.BlockSpec(memory_space=pltpu.VMEM)
ANY = pl.BlockSpec(memory_space=pltpu.HBM)
PARAMS = pltpu.CompilerParams(vmem_limit_bytes=VMEM_LIMIT)


def in_hbm(x):
    return pltpu.with_memory_space_constraint(x, pltpu.HBM)


def in_vmem(x):
    return pltpu.with_memory_space_constraint(x, pltpu.VMEM)


def cost(flops, moved, exps=0):
    return pl.CostEstimate(flops=flops, bytes_accessed=moved, transcendentals=exps)


MIX_BY_PERMUTE = False


def body(
    grid_tokens, obs_tokens, w_query, w_gridval, w_key, w_obsval, w_gridout, w_obsout, obs_count, home_block, seam_block
):
    tiles = lax.axis_size("tile")
    swap_a = [(i, i ^ 1) for i in range(tiles)]
    swap_b = [(i, (i + 1) % tiles if i % 2 else (i - 1) % tiles) for i in range(tiles)]
    f32, bf16 = jnp.float32, jnp.bfloat16
    pay_shape = pltpu.VMEM((PAY, BS), bf16)
    pay_b_shape = pltpu.VMEM((PAY_B, BS), bf16)
    acc_shape = pltpu.VMEM((4, HEADS, ROWS_O, BS), f32)
    top_shape = pltpu.VMEM((4, HEADS, 8, BS), f32)
    mix_shape = jax.ShapeDtypeStruct((PAIR, 128), bf16)
    mixes_shape = pltpu.HBM((GROUPS, PAIR, 128), bf16)
    w_shape = pltpu.HBM((GROUPS, WIDTH, D), bf16)
    out_shape = jax.ShapeDtypeStruct((128, D), bf16)

    pay_a, pay_b, w_spread = pl.pallas_call(
        project_kernel,
        out_shape=(pay_shape, pay_b_shape, w_shape),
        in_specs=[pl.BlockSpec(memory_space=pl.ANY)] + [ANY] * 10,
        out_specs=(VMEM, VMEM, ANY),
        scratch_shapes=[
            pltpu.VMEM((4 * BS, D), bf16),
            pltpu.VMEM((4 * WIDTH, D), bf16),
            pltpu.VMEM((WIDTH, D), bf16),
            pltpu.SMEM((2,), jnp.int32),
            pltpu.SMEM((2,), jnp.int32),
            pltpu.SMEM((1,), jnp.int32),
            pltpu.SemaphoreType.DMA((11 + GROUPS,)),
        ],
        compiler_params=PARAMS,
        cost_estimate=cost(1, 1),
    )(
        obs_count,
        *map(
            in_hbm,
            (home_block, seam_block, grid_tokens, obs_tokens, w_query.T, w_gridval.T, w_key.T, w_obsval.T, w_gridout, w_obsout),
        ),
    )
    w_own = lax.all_to_all(w_spread, "head", split_axis=0, concat_axis=0, tiled=True)
    rec_b = lax.ppermute(pay_b, "tile", swap_b)
    acc, top = pl.pallas_call(
        home_kernel,
        out_shape=(acc_shape, top_shape),
        in_specs=[VMEM] * 2,
        out_specs=(VMEM, VMEM),
        compiler_params=PARAMS,
        cost_estimate=cost(3 * 10**9, 1),
    )(pay_a, pay_b)
    pay_a2 = pay_a
    rec_a = lax.ppermute(pay_a2, "tile", swap_a)
    count = GROUPS if MIX_BY_PERMUTE else 1
    mixes = pl.pallas_call(
        seam_kernel,
        out_shape=((mix_shape,) * GROUPS if MIX_BY_PERMUTE else (mixes_shape,)) + (acc_shape, top_shape),
        in_specs=[VMEM] * 6,
        out_specs=(ANY,) + (VMEM,) * 2,
        input_output_aliases={4: count, 5: count + 1},
        scratch_shapes=[pltpu.VMEM(mixes_shape.shape, bf16), pltpu.SemaphoreType.DMA((2,))],
        compiler_params=PARAMS,
        cost_estimate=cost(1, 1),
    )(pay_a, pay_b, in_vmem(rec_a), in_vmem(rec_b), acc, top)
    late = mixes[0]
    late = mixes[0]
    if MIX_BY_PERMUTE:
        mixes = [mixes[0]] + [
            lax.ppermute(mixes[s], "head", [(i, (i + s) % GROUPS) for i in range(GROUPS)]) for s in (1, 2, 3)
        ]
    else:
        mixes = [lax.all_to_all(mixes[0], "head", split_axis=0, concat_axis=0, tiled=True)]
    w_own2, *_ = lax.optimization_barrier((w_own, late))
    w_other = lax.ppermute(w_own2, "tile", swap_a)
    own = pl.pallas_call(
        own_out_kernel,
        out_shape=pltpu.VMEM(out_shape.shape, bf16),
        in_specs=[VMEM] * 2,
        out_specs=VMEM,
        compiler_params=PARAMS,
        cost_estimate=cost(10**10, 1),
    )(in_vmem(mixes[0]), in_vmem(w_own))
    return pl.pallas_call(
        other_out_kernel,
        out_shape=(out_shape, out_shape),
        in_specs=[VMEM] * 3,
        out_specs=(VMEM, VMEM),
        compiler_params=PARAMS,
        cost_estimate=cost(1, 1),
    )(in_vmem(mixes[0]), in_vmem(w_other), own)


def solution(mesh):
    return jax.shard_map(
        body,
        mesh=mesh,
        in_specs=(
            P("tile", None),
            P("tile", None),
            P(None, "head"),
            P(None, "head"),
            P(None, "head"),
            P(None, "head"),
            P("head", None),
            P("head", None),
            P("tile"),
            P("tile"),
            P("tile"),
        ),
        out_specs=(P(("tile", "head"), None), P(("tile", "head"), None)),
        check_vma=False,
    )
```
